256 devices in a mesh: layer: 256 (over y, z, x, core).
Axes of the slice: x: 4, y: 4, z: 8, core: 2. Of those that a mesh axis runs over, the one named last changes fastest.
Arguments:
- inputs: float32 [128, 1024], replicated, may hold values from -1.5 to 1.5
- w_in: bfloat16 [256, 1024, 2048], P('layer'), may hold values from -0.28125 to 0.28125
- w_out: bfloat16 [256, 2048, 1024], P('layer'), may hold values from -0.397747564 to 0.397747564
Outputs:
- block_outputs: float32 [256, 128, 1024], P('layer')
The draws below stay inside these ranges and needn't reach their ends.
All inputs are finite; a program needn't handle non-finite values.
Results may differ from the reference program's by a relative error of at most 0.009.
Values sent between devices are 32-bit elements; how exact they have to be, the bound alone decides.
No kernel may reach another device: no remote copies, remote signals or barrier semaphores. Data moves between devices by JAX's collectives and lax.ppermute only.
A program may use at most 64 MiB of HBM per device.

```python
import math
import jax
import jax.numpy as jnp
from jax import lax

D = 1024
FF = 2048
ROWS = 128
CF = 8
NL = 256
NC = 32


def draw_w_in(key, part):
    key = jax.random.fold_in(key, 11)
    key_common, key_single = jax.random.split(key)
    common = jax.random.truncated_normal(key_common, -4.0, 4.0, (D, FF), jnp.float32)
    single = jax.random.truncated_normal(key_single, -4.0, 4.0, (NL, D, FF), jnp.float32)
    share = 0.8
    mixed = share * common[None] + math.sqrt(1.0 - share * share) * single
    return (mixed * (1.5 / math.sqrt(D))).astype(jnp.bfloat16)


def draw_w_out(key, part):
    key = jax.random.fold_in(key, 23)
    key_common, key_single = jax.random.split(key)
    common = jax.random.truncated_normal(key_common, -4.0, 4.0, (FF, D), jnp.float32)
    single = jax.random.truncated_normal(key_single, -4.0, 4.0, (NL, FF, D), jnp.float32)
    share = 0.8
    gain_value = 3.0
    mixed = share * common[None] + math.sqrt(1.0 - share * share) * single
    return (mixed * (gain_value / math.sqrt(FF))).astype(jnp.bfloat16)


def noise(rng, dims, scale, most, dtype=jnp.bfloat16):
    array = jax.random.normal(rng, dims, jnp.float32) * scale
    return jnp.minimum(jnp.maximum(array, -most), most).astype(dtype)


def setup_inputs(seed: int = 0) -> dict:
    arg_keys = jax.random.split(jax.random.key(seed), 4)
    inputs = noise(arg_keys[0], (ROWS, D), 0.25, 1.5, jnp.float32)
    w_in = draw_w_in(jax.random.fold_in(arg_keys[3], 71), 0)
    w_out = draw_w_out(jax.random.fold_in(arg_keys[3], 71), 0)
    return dict(inputs=inputs, w_in=w_in, w_out=w_out)


def increment(state, w_first, w_second):
    mean_sq = lax.optimization_barrier(jnp.mean(state * state, axis=-1, keepdims=True))
    normed = (state * lax.rsqrt(mean_sq + 1e-06)).astype(jnp.bfloat16)
    act = jax.nn.gelu(jnp.dot(normed, w_first, preferred_element_type=jnp.float32)).astype(jnp.bfloat16)
    return jnp.dot(act, w_second, preferred_element_type=jnp.float32)

def fine_sweep(cpoints, w_first, w_second, step):
    batched = jax.vmap(increment)
    states = [cpoints]
    made = []
    current = cpoints
    for j in range(CF - 1):
        current = current + step * batched(current, w_first[:, j], w_second[:, j])
        made.append(current)
        states.append(current)
    return (states, made)

def reference(inputs, w_in, w_out):
    step = 1.0 / NL
    coarse = CF * step
    batched = jax.vmap(increment)
    w_first = w_in.reshape(NC, CF, D, FF)
    w_second = w_out.reshape(NC, CF, FF, D)
    cpoints = jnp.broadcast_to(inputs[None], (NC, ROWS, D)).astype(jnp.float32)
    states, made = fine_sweep(cpoints, w_first, w_second, step)
    last = states[CF - 1]
    crossed = last + step * batched(last, w_first[:, CF - 1], w_second[:, CF - 1])
    cpoints = jnp.concatenate([inputs[None], crossed[:-1]], axis=0)
    states, made = fine_sweep(cpoints, w_first, w_second, step)
    last = states[CF - 1]
    fine = last + step * batched(last, w_first[:, CF - 1], w_second[:, CF - 1])
    psi = cpoints + coarse * batched(cpoints, w_first[:, 0], w_second[:, 0])

    def advance(carry, pieces):
        first, second, psi_here, fine_here = pieces
        moved = carry + coarse * increment(carry, first, second) - psi_here
        result = moved + fine_here
        return (result, result)
    start = inputs.astype(jnp.float32)
    final_carry, solved = lax.scan(advance, start, (w_first[:-1, 0], w_second[:-1, 0], psi[:-1], fine[:-1]))
    cpoints = jnp.concatenate([inputs[None], solved], axis=0)
    states, made = fine_sweep(cpoints, w_first, w_second, step)
    last = states[CF - 1]
    tail = last + step * batched(last, w_first[:, CF - 1], w_second[:, CF - 1])
    outputs = jnp.stack(made + [tail], axis=1)
    return outputs.reshape(NL, ROWS, D)
```

```python
import jax
import jax.numpy as jnp
from jax import lax
from jax.experimental import pallas as pl
from jax.experimental.pallas import tpu as pltpu
from jax.sharding import PartitionSpec as P

CF = 8
CHUNKS = 8
PROD, PSI, FINE = range(3)

VMEM = pl.BlockSpec(memory_space=pltpu.VMEM)
ANY = pl.BlockSpec(memory_space=pl.ANY)


def in_vmem(x):
    return pltpu.with_memory_space_constraint(x, pltpu.VMEM)


def load_kernel(inputs, w_in, w_out, held, first, second, store, sems):
    del store
    copies = [
        pltpu.make_async_copy(inputs, held, sems.at[0]),
        pltpu.make_async_copy(w_in.at[0], first, sems.at[1]),
        pltpu.make_async_copy(w_out.at[0], second, sems.at[2]),
    ]
    for copy in copies:
        copy.start()
    for copy in copies:
        copy.wait()


def load(inputs, w_in, w_out):
    rows, width = inputs.shape
    return pl.pallas_call(
        load_kernel,
        out_shape=(
            pltpu.VMEM((rows, width), jnp.float32),
            pltpu.VMEM(w_in.shape[1:], w_in.dtype),
            pltpu.VMEM(w_out.shape[1:], w_out.dtype),
            pltpu.VMEM((3, rows, width), jnp.float32),
        ),
        in_specs=[ANY] * 3,
        out_specs=(VMEM,) * 4,
        scratch_shapes=[pltpu.SemaphoreType.DMA((3,))],
        compiler_params=pltpu.CompilerParams(vmem_limit_bytes=4 * 2**20),
    )(*(pltpu.with_memory_space_constraint(x, pltpu.HBM) for x in (inputs, w_in, w_out)))


def increment(state, first, second):
    mean_sq = jnp.mean(state * state, axis=-1, keepdims=True)
    normed = (state * lax.rsqrt(mean_sq + 1e-06)).astype(jnp.bfloat16)
    hidden = jnp.dot(normed, first[...], preferred_element_type=jnp.float32)
    act = jax.nn.gelu(hidden).astype(jnp.bfloat16)
    return jnp.dot(act, second[...], preferred_element_type=jnp.float32)


class Plan:
    def __init__(self, points):
        self.points = points
        self.solve = 2 * CF
        self.last = self.solve + points - 3
        self.end = self.last + CF + CHUNKS - 1

    def first_pass(self, turn, interval, position):
        own = turn - position
        return (own >= 0) & (own < CHUNKS) & (interval < self.points - 2)

    def second_pass(self, turn, interval, position):
        own = turn - position - CF
        return (own >= 0) & (own < CHUNKS) & (interval >= 1) & (interval < self.points - 1)

    def solving(self, turn, interval, position):
        own = turn - self.solve - interval + 2
        return (position == 0) & (interval >= 2) & (own >= 0) & (own < CHUNKS)

    def last_pass(self, turn, interval, position):
        own = turn - self.last - position
        return (own >= 0) & (own < CHUNKS)

    def sends(self, turn):
        return turn < 2 * CF + CHUNKS - 1 or self.last <= turn < self.end - 1

    def solves_on(self, turn):
        return self.solve <= turn < self.last + CHUNKS - 1

    def next_pairs(self, turn):
        count = CF * self.points
        if CF - 1 <= turn < 2 * CF + CHUNKS - 1:
            return [(n, (n + 1) % count) for n in range(count)]
        return [(n, n - n % CF + (n + 1) % CF) for n in range(count)]

    def coarse_pairs(self, turn):
        first = self.solve + (turn - self.solve) // 2 * 2
        active = [
            k
            for k in range(2, self.points - 1)
            if self.solving(first, k, 0) or self.solving(first + 1, k, 0)
        ]
        low, high = CF * active[0], CF * (active[-1] + 1)
        target = {n: n ^ 1 for n in range(CF * self.points)}
        for head in range(low, high, CF):
            target[head] = head + CF
            target[head + CF + 1] = head + 1
        target[high] = high + 1
        target[low + 1] = low
        return sorted(target.items())


def stage(plan, turn, step, coarse, moved, coarse_moved, held, first, second, store):
    rows, width = held.shape
    part = rows // CHUNKS
    sends_next = plan.sends(turn)
    sends_coarse = plan.solves_on(turn)
    passes_one = turn < CF + CHUNKS - 1
    passes_two = CF <= turn < 2 * CF + CHUNKS - 1
    gathers = plan.solve <= turn < plan.solve + CHUNKS
    solves = plan.solve <= turn < plan.last + CHUNKS
    closes = turn >= plan.last
    reads_held = turn < CHUNKS
    operands = [first, second, store]
    reads_moved = moved is not None
    reads_coarse = coarse_moved is not None
    if reads_held:
        operands.append(held)
    if reads_moved:
        operands.append(moved)
    if reads_coarse:
        operands.append(coarse_moved)

    def kernel(*refs):
        refs = list(refs)
        first, second, _ = refs[:3]
        del refs[:3]
        held = refs.pop(0) if reads_held else None
        arrived = refs.pop(0) if reads_moved else None
        coarse_arrived = refs.pop(0) if reads_coarse else None
        store = refs.pop(0)
        sent = refs.pop(0) if sends_next else None
        coarse_sent = refs.pop(0) if sends_coarse else None
        state = refs.pop(0)

        index = lax.axis_index("layer")
        position = lax.rem(index, CF)
        interval = lax.div(index, CF)
        head = position == 0

        def chunk_rows(chunk):
            return pl.ds(pl.multiple_of(chunk * part, part), part)

        never = index < 0
        one = plan.first_pass(turn, interval, position) if passes_one else never
        two = plan.second_pass(turn, interval, position) if passes_two else never
        solving = plan.solving(turn, interval, position) if solves else never
        closing = plan.last_pass(turn, interval, position) if closes else never
        along = one | two | (closing & ~head)
        chunk = jnp.where(two, turn - position - CF, turn - position)
        if closes:
            chunk = jnp.where(head, chunk, turn - plan.last - position)
        if solves:
            chunk = jnp.where(solving, turn - plan.solve - interval + 2, chunk)

        if gathers:

            @pl.when(head)
            def _():
                store[FINE, (turn - plan.solve) * part : (turn - plan.solve + 1) * part, :] = arrived[...]

        if reads_held:

            @pl.when(head)
            def _():
                state[...] = held[turn * part : (turn + 1) * part, :]

        if reads_moved:

            @pl.when((along & ~head) | two)
            def _():
                state[...] = arrived[...]

        if solves:

            @pl.when(solving & (interval == 2))
            def _():
                state[...] = store[FINE, chunk_rows(chunk), :]

            if reads_coarse:

                @pl.when(solving & (interval > 2))
                def _():
                    state[...] = coarse_arrived[...] + store[FINE, chunk_rows(chunk), :]

        @pl.when(along | solving)
        def _():
            before = state[...]
            change = increment(before, first, second)
            after = before + step * change
            store[PROD, chunk_rows(chunk), :] = after
            if sends_next:
                sent[...] = after
            if passes_two:

                @pl.when(two & head)
                def _():
                    store[PSI, chunk_rows(chunk), :] = before + coarse * change

            if sends_coarse:

                @pl.when(solving)
                def _():
                    coarse_sent[...] = before + coarse * change - store[PSI, chunk_rows(chunk), :]

        if closes and turn < plan.last + CHUNKS:

            @pl.when(head)
            def _():
                own = turn - plan.last
                sent[...] = store[PROD, own * part : (own + 1) * part, :]

    small = pltpu.VMEM((part, width), jnp.float32)
    hidden = first.shape[1]
    results = pl.pallas_call(
        kernel,
        out_shape=(pltpu.VMEM(store.shape, store.dtype),) + (small,) * (sends_next + sends_coarse),
        in_specs=[VMEM] * len(operands),
        out_specs=(VMEM,) * (1 + sends_next + sends_coarse),
        scratch_shapes=[small],
        input_output_aliases={2: 0},
        compiler_params=pltpu.CompilerParams(vmem_limit_bytes=8 * 2**20),
        cost_estimate=pl.CostEstimate(
            flops=4 * part * width * hidden, bytes_accessed=4 * width * hidden, transcendentals=part * hidden
        ),
    )(*(in_vmem(x) for x in operands))
    store = results[0]
    moved = lax.ppermute(results[1], "layer", plan.next_pairs(turn)) if sends_next else None
    coarse_moved = lax.ppermute(results[-1], "layer", plan.coarse_pairs(turn)) if sends_coarse else None
    return moved, coarse_moved, store


def body(inputs, w_in, w_out):
    count = lax.axis_size("layer")
    plan = Plan(count // CF)
    step = 1.0 / count
    held, first, second, store = load(inputs, w_in, w_out)
    moved, coarse_moved = None, None
    for turn in range(plan.end):
        moved, coarse_moved, store = stage(
            plan, turn, step, CF * step, moved, coarse_moved, held, first, second, store
        )
    return store[PROD][None]


def solution(mesh):
    return jax.shard_map(
        body,
        mesh=mesh,
        in_specs=(P(), P("layer", None, None), P("layer", None, None)),
        out_specs=P("layer", None, None),
        check_vma=False,
    )
```

```python
import jax
import jax.numpy as jnp
from jax import lax
from jax.experimental import pallas as pl
from jax.experimental.pallas import tpu as pltpu
from jax.sharding import PartitionSpec as P

CF = 8
CHUNKS = 8
PROD, PSI, FINE = range(3)

VMEM = pl.BlockSpec(memory_space=pltpu.VMEM)
ANY = pl.BlockSpec(memory_space=pl.ANY)


def in_vmem(x):
    return pltpu.with_memory_space_constraint(x, pltpu.VMEM)


def load_kernel(inputs, w_in, w_out, held, first, second, store, sems):
    del store
    copies = [
        pltpu.make_async_copy(inputs, held, sems.at[0]),
        pltpu.make_async_copy(w_in.at[0], first, sems.at[1]),
        pltpu.make_async_copy(w_out.at[0], second, sems.at[2]),
    ]
    for copy in copies:
        copy.start()
    for copy in copies:
        copy.wait()


def load(inputs, w_in, w_out):
    rows, width = inputs.shape
    return pl.pallas_call(
        load_kernel,
        out_shape=(
            pltpu.VMEM((rows, width), jnp.float32),
            pltpu.VMEM(w_in.shape[1:], w_in.dtype),
            pltpu.VMEM(w_out.shape[1:], w_out.dtype),
            pltpu.VMEM((3, rows, width), jnp.float32),
        ),
        in_specs=[ANY] * 3,
        out_specs=(VMEM,) * 4,
        scratch_shapes=[pltpu.SemaphoreType.DMA((3,))],
        compiler_params=pltpu.CompilerParams(vmem_limit_bytes=4 * 2**20),
    )(*(pltpu.with_memory_space_constraint(x, pltpu.HBM) for x in (inputs, w_in, w_out)))


def increment(state, first, second):
    mean_sq = jnp.mean(state * state, axis=-1, keepdims=True)
    normed = (state * lax.rsqrt(mean_sq + 1e-06)).astype(jnp.bfloat16)
    hidden = jnp.dot(normed, first[...], preferred_element_type=jnp.float32)
    act = jax.nn.gelu(hidden).astype(jnp.bfloat16)
    return jnp.dot(act, second[...], preferred_element_type=jnp.float32)


class Plan:
    def __init__(self, points):
        self.points = points
        self.second = CF + 1
        self.gather = self.second + CF
        self.last = self.gather + points - 2
        self.end = self.last + CF + CHUNKS - 1

    def first_pass(self, turn, interval, position):
        own = turn - position
        return (own >= 0) & (own < CHUNKS) & (interval < self.points - 2)

    def second_pass(self, turn, interval, position):
        own = turn - position - self.second
        return (own >= 0) & (own < CHUNKS) & (interval >= 1) & (interval < self.points - 1)

    def solve_chunk(self, turn, interval):
        return turn - self.gather - interval + 1

    def solving(self, turn, interval, position):
        own = self.solve_chunk(turn, interval)
        return (position == 0) & (interval >= 2) & (own >= 0) & (own < CHUNKS)

    def last_pass(self, turn, interval, position):
        own = turn - self.last - position
        return (own >= 0) & (own < CHUNKS)

    def sends_along(self, turn):
        return turn < self.gather + CHUNKS - 1 or self.last <= turn < self.end - 1

    def relays(self, turn):
        return CF <= turn < CF + CHUNKS

    def solves_on(self, turn):
        return self.gather <= turn < self.last + CHUNKS - 1

    def along(self):
        return [(n, n - n % CF + (n + 1) % CF) for n in range(CF * self.points)]

    def across(self, turn):
        if self.relays(turn):
            low, high = 0, self.points - 1
        else:
            start = self.gather + (turn - self.gather) // 2 * 2
            low = max(1, start - self.gather - CHUNKS + 2)
            high = min(self.points - 1, start - self.gather + 3)
        target = {n: n ^ 1 for n in range(CF * self.points)}
        for head in range(CF * low, CF * high, CF):
            target[head] = head + CF
            target[head + CF + 1] = head + 1
        target[CF * high] = CF * high + 1
        target[CF * low + 1] = CF * low
        return sorted(target.items())


def stage(plan, turn, step, coarse, moved, coarse_moved, held, first, second, store):
    rows, width = held.shape
    part = rows // CHUNKS
    sends_along = plan.sends_along(turn)
    relays = plan.relays(turn)
    sends_across = relays or plan.solves_on(turn)
    passes_one = turn < CF + CHUNKS - 1
    passes_two = plan.second <= turn < plan.gather + CHUNKS - 1
    gathers = plan.gather <= turn < plan.gather + CHUNKS
    solves = plan.gather < turn < plan.last + CHUNKS
    closes = turn >= plan.last
    reads_held = turn < CHUNKS
    reads_moved = moved is not None
    reads_coarse = coarse_moved is not None
    operands = [first, second, store]
    if reads_held:
        operands.append(held)
    if reads_moved:
        operands.append(moved)
    if reads_coarse:
        operands.append(coarse_moved)

    def kernel(*refs):
        refs = list(refs)
        first, second, _ = refs[:3]
        del refs[:3]
        held = refs.pop(0) if reads_held else None
        arrived = refs.pop(0) if reads_moved else None
        coarse_arrived = refs.pop(0) if reads_coarse else None
        store = refs.pop(0)
        sent = refs.pop(0) if sends_along else None
        coarse_sent = refs.pop(0) if sends_across else None
        state = refs.pop(0)

        index = lax.axis_index("layer")
        position = lax.rem(index, CF)
        interval = lax.div(index, CF)
        head = position == 0

        def chunk_rows(chunk):
            return pl.ds(pl.multiple_of(chunk * part, part), part)

        def fixed_rows(chunk):
            return slice(chunk * part, (chunk + 1) * part)

        never = index < 0
        one = plan.first_pass(turn, interval, position) if passes_one else never
        two = plan.second_pass(turn, interval, position) if passes_two else never
        solving = plan.solving(turn, interval, position) if solves else never
        closing = plan.last_pass(turn, interval, position) & ~head if closes else never
        chunk = turn - position
        if passes_two:
            chunk = jnp.where(two, turn - position - plan.second, chunk)
        if closes:
            chunk = jnp.where(closing, turn - position - plan.last, chunk)
        if solves:
            chunk = jnp.where(solving, plan.solve_chunk(turn, interval), chunk)

        if gathers:

            @pl.when(head)
            def _():
                store[FINE, fixed_rows(turn - plan.gather), :] = arrived[...]

            @pl.when(head & (interval == 1))
            def _():
                coarse_sent[...] = arrived[...]

        if relays:

            @pl.when(head)
            def _():
                coarse_sent[...] = arrived[...]

        if reads_held:

            @pl.when(head)
            def _():
                state[...] = held[fixed_rows(turn), :]

        if reads_moved:

            @pl.when((one | two | closing) & ~head)
            def _():
                state[...] = arrived[...]

        if reads_coarse:

            @pl.when(solving | (two & head))
            def _():
                state[...] = coarse_arrived[...]

        @pl.when(one | two | closing | solving)
        def _():
            before = state[...]
            change = increment(before, first, second)
            after = before + step * change
            store[PROD, chunk_rows(chunk), :] = after
            if sends_along:
                sent[...] = after
            if passes_two:

                @pl.when(two & head)
                def _():
                    store[PSI, chunk_rows(chunk), :] = before + coarse * change

            if solves and sends_across:

                @pl.when(solving)
                def _():
                    coarse_sent[...] = (
                        before + coarse * change - store[PSI, chunk_rows(chunk), :]
                    ) + store[FINE, chunk_rows(chunk), :]

        if closes and turn < plan.last + CHUNKS:

            @pl.when(head)
            def _():
                sent[...] = store[PROD, fixed_rows(turn - plan.last), :]

    small = pltpu.VMEM((part, width), jnp.float32)
    hidden = first.shape[1]
    results = pl.pallas_call(
        kernel,
        out_shape=(pltpu.VMEM(store.shape, store.dtype),) + (small,) * (sends_along + sends_across),
        in_specs=[VMEM] * len(operands),
        out_specs=(VMEM,) * (1 + sends_along + sends_across),
        scratch_shapes=[small],
        input_output_aliases={2: 0},
        compiler_params=pltpu.CompilerParams(vmem_limit_bytes=8 * 2**20),
        cost_estimate=pl.CostEstimate(
            flops=4 * part * width * hidden, bytes_accessed=4 * width * hidden, transcendentals=part * hidden
        ),
    )(*(in_vmem(x) for x in operands))
    store = results[0]
    moved = lax.ppermute(results[1], "layer", plan.along()) if sends_along else None
    coarse_moved = lax.ppermute(results[-1], "layer", plan.across(turn)) if sends_across else None
    return moved, coarse_moved, store


def body(inputs, w_in, w_out):
    count = lax.axis_size("layer")
    plan = Plan(count // CF)
    step = 1.0 / count
    held, first, second, store = load(inputs, w_in, w_out)
    moved, coarse_moved = None, None
    for turn in range(plan.end):
        moved, coarse_moved, store = stage(
            plan, turn, step, CF * step, moved, coarse_moved, held, first, second, store
        )
    return store[PROD][None]


def solution(mesh):
    return jax.shard_map(
        body,
        mesh=mesh,
        in_specs=(P(), P("layer", None, None), P("layer", None, None)),
        out_specs=P("layer", None, None),
        check_vma=False,
    )
```

```python
import jax
import jax.numpy as jnp
import numpy as np
from jax import lax
from jax.experimental import pallas as pl
from jax.experimental.pallas import tpu as pltpu
from jax.sharding import PartitionSpec as P

CF = 8
CHUNKS = 4
GRID = (4, 8, 4, 2)
PROD, PSI, FINE, HOLD = range(4)
FULL_STOP = 1 << 20
WINDOW = 6

VMEM = pl.BlockSpec(memory_space=pltpu.VMEM)
ANY = pl.BlockSpec(memory_space=pl.ANY)


def in_vmem(x):
    return pltpu.with_memory_space_constraint(x, pltpu.VMEM)


def load_kernel(inputs, w_in, w_out, held, first, second, store, sems):
    del store
    copies = [
        pltpu.make_async_copy(inputs, held, sems.at[0]),
        pltpu.make_async_copy(w_in.at[0], first, sems.at[1]),
        pltpu.make_async_copy(w_out.at[0], second, sems.at[2]),
    ]
    for copy in copies:
        copy.start()
    for copy in copies:
        copy.wait()


def load(inputs, w_in, w_out):
    rows, width = inputs.shape
    return pl.pallas_call(
        load_kernel,
        out_shape=(
            pltpu.VMEM((rows, width), jnp.float32),
            pltpu.VMEM(w_in.shape[1:], w_in.dtype),
            pltpu.VMEM(w_out.shape[1:], w_out.dtype),
            pltpu.VMEM((4, rows, width), jnp.float32),
        ),
        in_specs=[ANY] * 3,
        out_specs=(VMEM,) * 4,
        scratch_shapes=[pltpu.SemaphoreType.DMA((3,))],
        compiler_params=pltpu.CompilerParams(vmem_limit_bytes=4 * 2**20),
    )(*(pltpu.with_memory_space_constraint(x, pltpu.HBM) for x in (inputs, w_in, w_out)))


def increment(state, first, second):
    mean_sq = jnp.mean(state * state, axis=-1, keepdims=True)
    normed = (state * lax.rsqrt(mean_sq + 1e-06)).astype(jnp.bfloat16)
    hidden = jnp.dot(normed, first[...], preferred_element_type=jnp.float32)
    act = jax.nn.gelu(hidden).astype(jnp.bfloat16)
    return jnp.dot(act, second[...], preferred_element_type=jnp.float32)


def pick(condition, yes, no):
    if isinstance(condition, (bool, np.bool_)):
        return yes if condition else no
    return jnp.where(condition, yes, no)


class Plan:
    def __init__(self, points):
        self.points = points
        self.solve = 2 * CF
        self.last = self.solve + points - 1
        self.end = self.last + CF + 2 * CHUNKS - 2

    def chunk(self, turn, start):
        own = turn - start
        return (own >= 0) & (own < 2 * CHUNKS) & (own & 1 == 0), own >> 1

    def first_start(self, interval):
        return pick((interval > 3) & (interval & 1 == 0), 1, 0)

    def relay_start(self, interval):
        return pick(interval < 3, CF, pick(interval & 1 == 1, CF + 1, CF + 2))

    def second_start(self, interval):
        late = pick(interval & 1 == 0, CF + 3, CF + 4)
        return pick(interval < 3, CF + 1, pick(interval == 3, CF + 2, late))

    def last_start(self, interval):
        early = (interval & 1 == 1) & (interval < self.points - 1)
        return pick(early, self.last - 1, self.last)

    def first_pass(self, turn, interval, position):
        due, own = self.chunk(turn, self.first_start(interval) + position)
        return due & (interval < self.points - 2), own

    def relay(self, turn, interval, position):
        due, own = self.chunk(turn, self.relay_start(interval))
        return due & (position == 0) & (interval < self.points - 2), own

    def second_pass(self, turn, interval, position):
        due, own = self.chunk(turn, self.second_start(interval) + position)
        return due & (interval >= 1) & (interval < self.points - 1), own

    def gather(self, turn, interval, position):
        due, own = self.chunk(turn, self.second_start(interval) + CF)
        return due & (position == 0) & (interval >= 1) & (interval < self.points - 1), own

    def solving(self, turn, interval, position):
        due, own = self.chunk(turn, self.solve + interval)
        return due & (position == 0) & (interval >= 2), own

    def last_pass(self, turn, interval, position):
        return self.chunk(turn, self.last_start(interval) + position)

    def needed(self, turn):
        target = {}
        settled = self.second_start(5) + CF + 2 * CHUNKS - 2
        window = range(turn, turn + 1)
        if turn >= settled:
            start = settled + (turn - settled) // WINDOW * WINDOW
            window = range(start + (turn - start) % 2, start + WINDOW, 2)
        for k in range(self.points):
            for p in range(CF - 1):
                if k == self.points - 1:
                    shown = turn >= self.last and (turn - self.last - p) % 2 == 0
                elif k > 2 or turn >= settled:
                    shown = (turn + k + p) % 2 == 1
                else:
                    shown = turn < CF and (turn - p) % 2 == 0
                one, two = self.first_pass(turn, k, p)[0], self.second_pass(turn, k, p)[0]
                if one or two or self.last_pass(turn, k, p)[0] or shown:
                    target[CF * k + p] = CF * k + p + 1
            here = CF * k + CF - 1
            if self.first_pass(turn, k, CF - 1)[0] or self.second_pass(turn, k, CF - 1)[0]:
                target[here] = CF * k
            across = any(self.solving(t, k, 0)[0] for t in window) or self.relay(turn, k, 0)[0]
            if k < self.points - 1 and (across or (k == 1 and self.gather(turn, k, 0)[0])):
                assert CF * k not in target or turn >= settled
                target[CF * k] = CF * (k + 1)
        return target

    def pairs(self, turn):
        target = self.needed(turn)
        count = CF * self.points
        assert len(set(target.values())) == len(target)
        sources = [n for n in range(count) if n not in target]
        goals = sorted(set(range(count)) - set(target.values()))
        for row, column in enumerate(assign(hops(sources, goals))):
            target[sources[row]] = goals[column]
        return sorted(target.items())


def hops(sources, goals):
    a = np.stack(np.unravel_index(np.array(sources), GRID))[:, :, None]
    b = np.stack(np.unravel_index(np.array(goals), GRID))[:, None, :]
    cost = 0.3 * (a[3] != b[3])
    for axis in range(3):
        gap = np.abs(a[axis] - b[axis])
        cost = cost + np.minimum(gap, GRID[axis] - gap)
        cost = cost + 0.4 * (a[axis] // 4 != b[axis] // 4) + 0.4 * (gap == 3) * (GRID[axis] == 4)
    cost = np.where(cost > 1.5, 3 * cost, cost)
    return np.where(np.array(sources)[:, None] == np.array(goals)[None], FULL_STOP, cost)


def assign(cost):
    size = len(cost)
    rows, columns = np.zeros(size + 1), np.zeros(size + 1)
    match = np.zeros(size + 1, int)
    for row in range(1, size + 1):
        match[0], column = row, 0
        least, way, used = np.full(size + 1, np.inf), np.zeros(size + 1, int), np.zeros(size + 1, bool)
        while True:
            used[column] = True
            at = match[column]
            reduced = cost[at - 1] - rows[at] - columns[1:]
            better = ~used[1:] & (reduced < least[1:])
            least[1:][better] = reduced[better]
            way[1:][better] = column
            following = int(np.argmin(np.where(used, np.inf, least)))
            step = least[following]
            rows[match[used]] += step
            columns[used] -= step
            least[~used] -= step
            column = following
            if match[column] == 0:
                break
        while column:
            match[column] = match[way[column]]
            column = way[column]
    result = np.zeros(size, int)
    result[match[1:] - 1] = np.arange(size)
    return result


def stage(plan, turn, step, coarse, moved, held, first, second, store):
    rows, width = held.shape
    part = rows // CHUNKS
    places = [(k, p) for k in range(plan.points) for p in range(CF)]

    def happens(what):
        return any(what(turn, k, p)[0] for k, p in places)

    sends = turn < plan.end - 1
    has_one, has_two = happens(plan.first_pass), happens(plan.second_pass)
    has_relay, has_gather = happens(plan.relay), happens(plan.gather)
    has_solving, has_last = happens(plan.solving), happens(plan.last_pass)
    reads_held = has_one and turn < 2 * CHUNKS
    reads_moved = moved is not None
    holds = CF <= turn < CF + 2 * CHUNKS + 2
    operands = [first, second, store] + [held] * reads_held + [moved] * reads_moved

    def kernel(*refs):
        refs = list(refs)
        first, second, _ = refs[:3]
        del refs[:3]
        held = refs.pop(0) if reads_held else None
        arrived = refs.pop(0) if reads_moved else None
        store = refs.pop(0)
        sent = refs.pop(0) if sends else None
        state = refs.pop(0)

        index = lax.axis_index("layer")
        position = index & (CF - 1)
        interval = lax.div(index, CF)
        head = position == 0
        late = interval > 2
        never = (index < 0, 0)
        place = (turn, interval, position)
        one, chunk = plan.first_pass(*place) if has_one else never
        two, own = plan.second_pass(*place) if has_two else never
        chunk = jnp.where(two, own, chunk)
        solving, own = plan.solving(*place) if has_solving else never
        chunk = jnp.where(solving, own, chunk)
        last, last_chunk = plan.last_pass(*place) if has_last else never
        closing = last & ~head
        chunk = jnp.where(closing, last_chunk, chunk)

        def chunk_rows(chunk):
            return pl.ds(pl.multiple_of(chunk * part, part), part)

        if has_relay:
            relay, _ = plan.relay(*place)

            @pl.when(relay & ~late)
            def _():
                sent[...] = arrived[...]

            @pl.when(relay & late)
            def _():
                sent[...] = store[HOLD, :part, :]

        if has_gather:
            gather, own = plan.gather(*place)

            @pl.when(gather)
            def _():
                store[FINE, chunk_rows(own), :] = arrived[...]

            @pl.when(gather & (interval == 1))
            def _():
                sent[...] = arrived[...]

        if reads_held:

            @pl.when(one & head)
            def _():
                state[...] = held[chunk_rows(chunk), :]

        if reads_moved:

            @pl.when((one & ~head) | (two & ~(head & late)) | closing | solving)
            def _():
                state[...] = arrived[...]

        if has_two:

            @pl.when(two & head & late)
            def _():
                state[...] = store[HOLD, :part, :]

        if holds:

            @pl.when(head & late)
            def _():
                store[HOLD, :part, :] = arrived[...]

        @pl.when(one | two | closing | solving)
        def _():
            before = state[...]
            change = increment(before, first, second)
            after = before + step * change
            store[PROD, chunk_rows(chunk), :] = after
            if sends:
                sent[...] = after
            if has_two:

                @pl.when(two & head)
                def _():
                    store[PSI, chunk_rows(chunk), :] = before + coarse * change

            if has_solving:

                @pl.when(solving & (interval < plan.points - 1))
                def _():
                    sent[...] = (before + coarse * change - store[PSI, chunk_rows(chunk), :]) + store[
                        FINE, chunk_rows(chunk), :
                    ]

        if has_last and sends:

            @pl.when(last & head)
            def _():
                sent[...] = store[PROD, chunk_rows(last_chunk), :]

    small = pltpu.VMEM((part, width), jnp.float32)
    hidden = first.shape[1]
    results = pl.pallas_call(
        kernel,
        out_shape=(pltpu.VMEM(store.shape, store.dtype),) + (small,) * sends,
        in_specs=[VMEM] * len(operands),
        out_specs=(VMEM,) * (1 + sends),
        scratch_shapes=[small],
        input_output_aliases={2: 0},
        compiler_params=pltpu.CompilerParams(vmem_limit_bytes=8 * 2**20),
        cost_estimate=pl.CostEstimate(
            flops=4 * part * width * hidden, bytes_accessed=4 * width * hidden, transcendentals=part * hidden
        ),
    )(*(in_vmem(x) for x in operands))
    moved = lax.ppermute(results[1], "layer", plan.pairs(turn)) if sends else None
    return moved, results[0]


def body(inputs, w_in, w_out):
    count = lax.axis_size("layer")
    plan = Plan(count // CF)
    step = 1.0 / count
    held, first, second, store = load(inputs, w_in, w_out)
    moved = None
    for turn in range(plan.end):
        moved, store = stage(plan, turn, step, CF * step, moved, held, first, second, store)
    return store[PROD][None]


def solution(mesh):
    return jax.shard_map(
        body,
        mesh=mesh,
        in_specs=(P(), P("layer", None, None), P("layer", None, None)),
        out_specs=P("layer", None, None),
        check_vma=False,
    )
```

```python
import jax
import jax.numpy as jnp
from jax import lax
from jax.experimental import pallas as pl
from jax.experimental.pallas import tpu as pltpu
from jax.sharding import PartitionSpec as P

CF = 8
CHUNKS = 4
WINDOW = 4
PROD, PSI, FINE = range(3)

VMEM = pl.BlockSpec(memory_space=pltpu.VMEM)
ANY = pl.BlockSpec(memory_space=pl.ANY)


def in_vmem(x):
    return pltpu.with_memory_space_constraint(x, pltpu.VMEM)


def load_kernel(inputs, w_in, w_out, held, first, second, store, sems):
    del store
    copies = [
        pltpu.make_async_copy(inputs, held, sems.at[0]),
        pltpu.make_async_copy(w_in.at[0], first, sems.at[1]),
        pltpu.make_async_copy(w_out.at[0], second, sems.at[2]),
    ]
    for copy in copies:
        copy.start()
    for copy in copies:
        copy.wait()


def load(inputs, w_in, w_out):
    rows, width = inputs.shape
    return pl.pallas_call(
        load_kernel,
        out_shape=(
            pltpu.VMEM((rows, width), jnp.float32),
            pltpu.VMEM(w_in.shape[1:], w_in.dtype),
            pltpu.VMEM(w_out.shape[1:], w_out.dtype),
            pltpu.VMEM((3, rows, width), jnp.float32),
        ),
        in_specs=[ANY] * 3,
        out_specs=(VMEM,) * 4,
        scratch_shapes=[pltpu.SemaphoreType.DMA((3,))],
        compiler_params=pltpu.CompilerParams(vmem_limit_bytes=4 * 2**20),
    )(*(pltpu.with_memory_space_constraint(x, pltpu.HBM) for x in (inputs, w_in, w_out)))


def increment(state, first, second):
    mean_sq = jnp.mean(state * state, axis=-1, keepdims=True)
    normed = (state * lax.rsqrt(mean_sq + 1e-06)).astype(jnp.bfloat16)
    hidden = jnp.dot(normed, first[...], preferred_element_type=jnp.float32)
    act = jax.nn.gelu(hidden).astype(jnp.bfloat16)
    return jnp.dot(act, second[...], preferred_element_type=jnp.float32)


class Plan:
    def __init__(self, points):
        self.points = points
        self.solve = 2 * CF
        self.last = self.solve + points - 3
        self.end = self.last + CF + 2 * CHUNKS - 2

    def chunk(self, turn, start):
        own = turn - start
        return (own >= 0) & (own < 2 * CHUNKS) & (own & 1 == 0), own >> 1

    def first_pass(self, turn, interval, position):
        due, own = self.chunk(turn, position)
        return due & (interval < self.points - 2), own

    def second_pass(self, turn, interval, position):
        due, own = self.chunk(turn, position + CF)
        return due & (interval >= 1) & (interval < self.points - 1), own

    def solving(self, turn, interval, position):
        due, own = self.chunk(turn, self.solve + interval - 2)
        return due & (position == 0) & (interval >= 2), own

    def last_pass(self, turn, interval, position):
        return self.chunk(turn, self.last + position)

    def sends_along(self, turn):
        return turn < self.solve + 2 * CHUNKS - 2 or self.last <= turn < self.end - 1

    def sends_across(self, turn):
        return self.solve <= turn < self.last + 2 * CHUNKS - 2

    def along(self, turn):
        count = CF * self.points
        if CF - 1 <= turn < self.last and turn % 2:
            return [(n, (n + 1) % count) for n in range(count)]
        target = {n: n ^ 1 for n in range(count)}
        if (turn - self.last * (turn >= self.last)) % 2:
            for k in range(self.points):
                for p in range(1, CF - 1, 2):
                    target[CF * k + p] = CF * k + p + 1
                    target[CF * k + p + 1] = CF * k + p
                for p in (0, CF - 1):
                    target[CF * k + p] = CF * (k ^ 1) + p
        return sorted(target.items())

    def across(self, turn):
        start = self.solve + (turn - self.solve) // WINDOW * WINDOW
        target = {n: n ^ 1 for n in range(CF * self.points)}
        for k in range(2, self.points - 1):
            if any(self.solving(t, k, 0)[0] for t in range(start + (turn - start) % 2, start + WINDOW, 2)):
                for here in (CF * k, CF * k + 1):
                    target[here], target[here + CF] = here + CF, here
        return sorted(target.items())


def stage(plan, turn, step, coarse, moved, coarse_moved, held, first, second, store):
    rows, width = held.shape
    part = rows // CHUNKS
    sends_along, sends_across = plan.sends_along(turn), plan.sends_across(turn)
    passes_one = turn < CF + 2 * CHUNKS - 2
    passes_two = CF <= turn < 2 * CF + 2 * CHUNKS - 2
    gathers = plan.solve <= turn < plan.solve + 2 * CHUNKS and turn % 2 == 0
    solves = plan.solve <= turn < plan.last + 2 * CHUNKS - 1
    closes = turn >= plan.last
    reads_held = turn < 2 * CHUNKS and turn % 2 == 0
    reads_moved = moved is not None
    reads_coarse = coarse_moved is not None
    operands = [first, second, store]
    if reads_held:
        operands.append(held)
    if reads_moved:
        operands.append(moved)
    if reads_coarse:
        operands.append(coarse_moved)

    def kernel(*refs):
        refs = list(refs)
        first, second, _ = refs[:3]
        del refs[:3]
        held = refs.pop(0) if reads_held else None
        arrived = refs.pop(0) if reads_moved else None
        coarse_arrived = refs.pop(0) if reads_coarse else None
        store = refs.pop(0)
        sent = refs.pop(0) if sends_along else None
        coarse_sent = refs.pop(0) if sends_across else None
        state = refs.pop(0)

        index = lax.axis_index("layer")
        position = index & (CF - 1)
        interval = lax.div(index, CF)
        head = position == 0

        def chunk_rows(chunk):
            return pl.ds(pl.multiple_of(chunk * part, part), part)

        def fixed_rows(chunk):
            return slice(chunk * part, (chunk + 1) * part)

        place = (turn, interval, position)
        never = (index < 0, 0)
        one, chunk = plan.first_pass(*place) if passes_one else never
        two, own = plan.second_pass(*place) if passes_two else never
        chunk = jnp.where(two, own, chunk)
        solving, own = plan.solving(*place) if solves else never
        chunk = jnp.where(solving, own, chunk)
        last, last_chunk = plan.last_pass(*place) if closes else never
        closing = last & ~head
        chunk = jnp.where(closing, last_chunk, chunk)

        if gathers:

            @pl.when(head)
            def _():
                store[FINE, fixed_rows((turn - plan.solve) // 2), :] = arrived[...]

        if reads_held:

            @pl.when(head)
            def _():
                state[...] = held[fixed_rows(turn // 2), :]

        if reads_moved:

            @pl.when((one & ~head) | two | closing)
            def _():
                state[...] = arrived[...]

        if solves:

            @pl.when(solving & (interval == 2))
            def _():
                state[...] = store[FINE, chunk_rows(chunk), :]

        if reads_coarse:

            @pl.when(solving & (interval > 2))
            def _():
                state[...] = coarse_arrived[...] + store[FINE, chunk_rows(chunk), :]

        @pl.when(one | two | closing | solving)
        def _():
            before = state[...]
            change = increment(before, first, second)
            after = before + step * change
            store[PROD, chunk_rows(chunk), :] = after
            if sends_along:
                sent[...] = after
            if passes_two:

                @pl.when(two & head)
                def _():
                    store[PSI, chunk_rows(chunk), :] = before + coarse * change

            if sends_across:

                @pl.when(solving)
                def _():
                    coarse_sent[...] = before + coarse * change - store[PSI, chunk_rows(chunk), :]

        if closes and sends_along:

            @pl.when(last & head)
            def _():
                sent[...] = store[PROD, chunk_rows(last_chunk), :]

    small = pltpu.VMEM((part, width), jnp.float32)
    hidden = first.shape[1]
    results = pl.pallas_call(
        kernel,
        out_shape=(pltpu.VMEM(store.shape, store.dtype),) + (small,) * (sends_along + sends_across),
        in_specs=[VMEM] * len(operands),
        out_specs=(VMEM,) * (1 + sends_along + sends_across),
        scratch_shapes=[small],
        input_output_aliases={2: 0},
        compiler_params=pltpu.CompilerParams(vmem_limit_bytes=8 * 2**20),
        cost_estimate=pl.CostEstimate(
            flops=4 * part * width * hidden, bytes_accessed=4 * width * hidden, transcendentals=part * hidden
        ),
    )(*(in_vmem(x) for x in operands))
    store = results[0]
    moved = lax.ppermute(results[1], "layer", plan.along(turn)) if sends_along else None
    coarse_moved = lax.ppermute(results[-1], "layer", plan.across(turn)) if sends_across else None
    return moved, coarse_moved, store


def body(inputs, w_in, w_out):
    count = lax.axis_size("layer")
    plan = Plan(count // CF)
    step = 1.0 / count
    held, first, second, store = load(inputs, w_in, w_out)
    moved, coarse_moved = None, None
    for turn in range(plan.end):
        moved, coarse_moved, store = stage(
            plan, turn, step, CF * step, moved, coarse_moved, held, first, second, store
        )
    return store[PROD][None]


def solution(mesh):
    return jax.shard_map(
        body,
        mesh=mesh,
        in_specs=(P(), P("layer", None, None), P("layer", None, None)),
        out_specs=P("layer", None, None),
        check_vma=False,
    )
```

```python
import jax
import jax.numpy as jnp
from jax import lax
from jax.experimental import pallas as pl
from jax.experimental.pallas import tpu as pltpu
from jax.sharding import PartitionSpec as P

CF = 8
CHUNKS = 4
WINDOW = 4
PROD, PSI, FINE = range(3)

VMEM = pl.BlockSpec(memory_space=pltpu.VMEM)
ANY = pl.BlockSpec(memory_space=pl.ANY)


def in_vmem(x):
    return pltpu.with_memory_space_constraint(x, pltpu.VMEM)


def load_kernel(inputs, w_in, w_out, held, first, second, store, sems):
    del store
    copies = [
        pltpu.make_async_copy(inputs, held, sems.at[0]),
        pltpu.make_async_copy(w_in.at[0], first, sems.at[1]),
        pltpu.make_async_copy(w_out.at[0], second, sems.at[2]),
    ]
    for copy in copies:
        copy.start()
    for copy in copies:
        copy.wait()


def load(inputs, w_in, w_out):
    rows, width = inputs.shape
    return pl.pallas_call(
        load_kernel,
        out_shape=(
            pltpu.VMEM((rows, width), jnp.float32),
            pltpu.VMEM(w_in.shape[1:], w_in.dtype),
            pltpu.VMEM(w_out.shape[1:], w_out.dtype),
            pltpu.VMEM((3, rows, width), jnp.float32),
        ),
        in_specs=[ANY] * 3,
        out_specs=(VMEM,) * 4,
        scratch_shapes=[pltpu.SemaphoreType.DMA((3,))],
        compiler_params=pltpu.CompilerParams(vmem_limit_bytes=4 * 2**20),
    )(*(pltpu.with_memory_space_constraint(x, pltpu.HBM) for x in (inputs, w_in, w_out)))


def increment(state, first, second):
    mean_sq = jnp.mean(state * state, axis=-1, keepdims=True)
    normed = (state * lax.rsqrt(mean_sq + 1e-06)).astype(jnp.bfloat16)
    hidden = jnp.dot(normed, first[...], preferred_element_type=jnp.float32)
    act = jax.nn.gelu(hidden).astype(jnp.bfloat16)
    return jnp.dot(act, second[...], preferred_element_type=jnp.float32)


class Plan:
    def __init__(self, points):
        self.points = points
        self.solve = 2 * CF
        self.last = self.solve + points - 3
        self.end = self.last + CF + 2 * CHUNKS - 2

    def chunk(self, turn, start):
        own = turn - start
        return (own >= 0) & (own < 2 * CHUNKS) & (own & 1 == 0), own >> 1

    def first_pass(self, turn, interval, position):
        due, own = self.chunk(turn, position)
        return due & (interval < self.points - 2), own

    def second_pass(self, turn, interval, position):
        due, own = self.chunk(turn, position + CF)
        return due & (interval >= 1) & (interval < self.points - 1), own

    def solving(self, turn, interval, position):
        due, own = self.chunk(turn, self.solve + interval - 2)
        return due & (position == 0) & (interval >= 2), own

    def last_pass(self, turn, interval, position):
        return self.chunk(turn, self.last + position)

    def sends_along(self, turn):
        return turn < self.solve + 2 * CHUNKS - 2 or self.last <= turn < self.end - 1

    def sends_across(self, turn):
        return self.solve <= turn < self.last + 2 * CHUNKS - 2

    def along(self, turn):
        count = CF * self.points
        if CF - 1 <= turn < self.last and turn % 2:
            return [(n, (n + 1) % count) for n in range(count)]
        target = {n: n ^ 1 for n in range(count)}
        if (turn - self.last * (turn >= self.last)) % 2:
            for k in range(self.points):
                for p in range(1, CF - 1, 2):
                    target[CF * k + p] = CF * k + p + 1
                    target[CF * k + p + 1] = CF * k + p
                for p in (0, CF - 1):
                    target[CF * k + p] = CF * (k ^ 1) + p
        return sorted(target.items())

    def across(self, turn):
        start = self.solve + (turn - self.solve) // WINDOW * WINDOW
        target = {n: n ^ 1 for n in range(CF * self.points)}
        for k in range(2, self.points - 1):
            if any(self.solving(t, k, 0)[0] for t in range(start + (turn - start) % 2, start + WINDOW, 2)):
                here, there = CF * k, CF * (k + 1)
                target.update({here: there, there: there + 1, there + 1: here + 1, here + 1: here})
        return sorted(target.items())


def stage(plan, turn, step, coarse, moved, coarse_moved, held, first, second, store):
    rows, width = held.shape
    part = rows // CHUNKS
    sends_along, sends_across = plan.sends_along(turn), plan.sends_across(turn)
    passes_one = turn < CF + 2 * CHUNKS - 2
    passes_two = CF <= turn < 2 * CF + 2 * CHUNKS - 2
    gathers = plan.solve <= turn < plan.solve + 2 * CHUNKS and turn % 2 == 0
    solves = plan.solve <= turn < plan.last + 2 * CHUNKS - 1
    closes = turn >= plan.last
    reads_held = turn < 2 * CHUNKS and turn % 2 == 0
    reads_moved = moved is not None
    reads_coarse = coarse_moved is not None
    operands = [first, second, store]
    if reads_held:
        operands.append(held)
    if reads_moved:
        operands.append(moved)
    if reads_coarse:
        operands.append(coarse_moved)

    def kernel(*refs):
        refs = list(refs)
        first, second, _ = refs[:3]
        del refs[:3]
        held = refs.pop(0) if reads_held else None
        arrived = refs.pop(0) if reads_moved else None
        coarse_arrived = refs.pop(0) if reads_coarse else None
        store = refs.pop(0)
        sent = refs.pop(0) if sends_along else None
        coarse_sent = refs.pop(0) if sends_across else None
        state = refs.pop(0)

        index = lax.axis_index("layer")
        position = index & (CF - 1)
        interval = lax.div(index, CF)
        head = position == 0

        def chunk_rows(chunk):
            return pl.ds(pl.multiple_of(chunk * part, part), part)

        def fixed_rows(chunk):
            return slice(chunk * part, (chunk + 1) * part)

        place = (turn, interval, position)
        never = (index < 0, 0)
        one, chunk = plan.first_pass(*place) if passes_one else never
        two, own = plan.second_pass(*place) if passes_two else never
        chunk = jnp.where(two, own, chunk)
        solving, own = plan.solving(*place) if solves else never
        chunk = jnp.where(solving, own, chunk)
        last, last_chunk = plan.last_pass(*place) if closes else never
        closing = last & ~head
        chunk = jnp.where(closing, last_chunk, chunk)

        if gathers:

            @pl.when(head)
            def _():
                store[FINE, fixed_rows((turn - plan.solve) // 2), :] = arrived[...]

        if reads_held:

            @pl.when(head)
            def _():
                state[...] = held[fixed_rows(turn // 2), :]

        if reads_moved:

            @pl.when((one & ~head) | two | closing)
            def _():
                state[...] = arrived[...]

        if solves:

            @pl.when(solving & (interval == 2))
            def _():
                state[...] = store[FINE, chunk_rows(chunk), :]

        if reads_coarse:

            @pl.when(solving & (interval > 2))
            def _():
                state[...] = coarse_arrived[...] + store[FINE, chunk_rows(chunk), :]

        @pl.when(one | two | closing | solving)
        def _():
            before = state[...]
            change = increment(before, first, second)
            after = before + step * change
            store[PROD, chunk_rows(chunk), :] = after
            if sends_along:
                sent[...] = after
            if passes_two:

                @pl.when(two & head)
                def _():
                    store[PSI, chunk_rows(chunk), :] = before + coarse * change

            if sends_across:

                @pl.when(solving)
                def _():
                    coarse_sent[...] = before + coarse * change - store[PSI, chunk_rows(chunk), :]

        if closes and sends_along:

            @pl.when(last & head)
            def _():
                sent[...] = store[PROD, chunk_rows(last_chunk), :]

    small = pltpu.VMEM((part, width), jnp.float32)
    hidden = first.shape[1]
    results = pl.pallas_call(
        kernel,
        out_shape=(pltpu.VMEM(store.shape, store.dtype),) + (small,) * (sends_along + sends_across),
        in_specs=[VMEM] * len(operands),
        out_specs=(VMEM,) * (1 + sends_along + sends_across),
        scratch_shapes=[small],
        input_output_aliases={2: 0},
        compiler_params=pltpu.CompilerParams(vmem_limit_bytes=8 * 2**20),
        cost_estimate=pl.CostEstimate(
            flops=4 * part * width * hidden, bytes_accessed=4 * width * hidden, transcendentals=part * hidden
        ),
    )(*(in_vmem(x) for x in operands))
    store = results[0]
    moved = lax.ppermute(results[1], "layer", plan.along(turn)) if sends_along else None
    coarse_moved = lax.ppermute(results[-1], "layer", plan.across(turn)) if sends_across else None
    return moved, coarse_moved, store


def body(inputs, w_in, w_out):
    count = lax.axis_size("layer")
    plan = Plan(count // CF)
    step = 1.0 / count
    held, first, second, store = load(inputs, w_in, w_out)
    moved, coarse_moved = None, None
    for turn in range(plan.end):
        moved, coarse_moved, store = stage(
            plan, turn, step, CF * step, moved, coarse_moved, held, first, second, store
        )
    return store[PROD][None]


def solution(mesh):
    return jax.shard_map(
        body,
        mesh=mesh,
        in_specs=(P(), P("layer", None, None), P("layer", None, None)),
        out_specs=P("layer", None, None),
        check_vma=False,
    )
```

```python
import jax
import jax.numpy as jnp
from jax import lax
from jax.experimental import pallas as pl
from jax.experimental.pallas import tpu as pltpu
from jax.sharding import PartitionSpec as P

CF = 8
CHUNKS = 4
HALVES = 2
WINDOW = 6
PROD, PSI, FINE = range(3)

VMEM = pl.BlockSpec(memory_space=pltpu.VMEM)
ANY = pl.BlockSpec(memory_space=pl.ANY)


def in_vmem(x):
    return pltpu.with_memory_space_constraint(x, pltpu.VMEM)


def load_kernel(inputs, w_in, w_out, held, first, second, store, sems):
    del store
    copies = [
        pltpu.make_async_copy(inputs, held, sems.at[0]),
        pltpu.make_async_copy(w_in.at[0], first, sems.at[1]),
        pltpu.make_async_copy(w_out.at[0], second, sems.at[2]),
    ]
    for copy in copies:
        copy.start()
    for copy in copies:
        copy.wait()


def load(inputs, w_in, w_out):
    rows, width = inputs.shape
    return pl.pallas_call(
        load_kernel,
        out_shape=(
            pltpu.VMEM((rows, width), jnp.float32),
            pltpu.VMEM(w_in.shape[1:], w_in.dtype),
            pltpu.VMEM(w_out.shape[1:], w_out.dtype),
            pltpu.VMEM((3, rows, width), jnp.float32),
        ),
        in_specs=[ANY] * 3,
        out_specs=(VMEM,) * 4,
        scratch_shapes=[pltpu.SemaphoreType.DMA((3,))],
        compiler_params=pltpu.CompilerParams(vmem_limit_bytes=4 * 2**20),
    )(*(pltpu.with_memory_space_constraint(x, pltpu.HBM) for x in (inputs, w_in, w_out)))


def increment(state, first, second):
    mean_sq = jnp.mean(state * state, axis=-1, keepdims=True)
    normed = (state * lax.rsqrt(mean_sq + 1e-06)).astype(jnp.bfloat16)
    hidden = jnp.dot(normed, first[...], preferred_element_type=jnp.float32)
    act = jax.nn.gelu(hidden).astype(jnp.bfloat16)
    return jnp.dot(act, second[...], preferred_element_type=jnp.float32)


class Plan:
    def __init__(self, points):
        self.points = points
        self.solve = 2 * CF
        self.last = self.solve + points - 3
        self.end = self.last + CF + 2 * CHUNKS - 2

    def chunk(self, turn, start):
        own = turn - start
        return (own >= 0) & (own < 2 * CHUNKS) & (own & 1 == 0), own >> 1

    def first_pass(self, turn, interval, position):
        due, own = self.chunk(turn, position)
        return due & (interval < self.points - 2), own

    def second_pass(self, turn, interval, position):
        due, own = self.chunk(turn, position + CF)
        return due & (interval >= 1) & (interval < self.points - 1), own

    def solving(self, turn, interval, position):
        due, own = self.chunk(turn, self.solve + interval - 2)
        return due & (position == 0) & (interval >= 2), own

    def last_pass(self, turn, interval, position):
        return self.chunk(turn, self.last + position)

    def sends_along(self, turn):
        return turn < self.solve + 2 * CHUNKS - 2 or self.last <= turn < self.end - 1

    def sends_across(self, turn):
        return self.solve <= turn < self.last + 2 * CHUNKS - 2

    def along(self, turn):
        count = CF * self.points
        if CF - 1 <= turn < self.last and turn % 2:
            return [(n, (n + 1) % count) for n in range(count)]
        target = {n: n ^ 1 for n in range(count)}
        if (turn - self.last * (turn >= self.last)) % 2:
            for k in range(self.points):
                for p in range(1, CF - 1, 2):
                    target[CF * k + p] = CF * k + p + 1
                    target[CF * k + p + 1] = CF * k + p
                for p in (0, CF - 1):
                    target[CF * k + p] = CF * (k ^ 1) + p
        return sorted(target.items())

    def across(self, turn):
        start = self.solve + (turn - self.solve) // WINDOW * WINDOW
        target = {n: n ^ 1 for n in range(CF * self.points)}
        for k in range(2, self.points - 1):
            if any(self.solving(t, k, 0)[0] for t in range(start + (turn - start) % 2, start + WINDOW, 2)):
                here, there = CF * k, CF * (k + 1)
                target.update({here: there, there: there + 1, there + 1: here + 1, here + 1: here})
        return sorted(target.items())


def stage(plan, turn, half, step, coarse, moved, coarse_moved, held, first, second, store):
    rows, width = held.shape
    part = rows // CHUNKS // HALVES
    sends_along, sends_across = plan.sends_along(turn), plan.sends_across(turn)
    passes_one = turn < CF + 2 * CHUNKS - 2
    passes_two = CF <= turn < 2 * CF + 2 * CHUNKS - 2
    gathers = plan.solve <= turn < plan.solve + 2 * CHUNKS and turn % 2 == 0
    solves = plan.solve <= turn < plan.last + 2 * CHUNKS - 1
    closes = turn >= plan.last
    reads_held = turn < 2 * CHUNKS and turn % 2 == 0
    reads_moved = moved is not None
    reads_coarse = coarse_moved is not None
    operands = [first, second, store]
    if reads_held:
        operands.append(held)
    if reads_moved:
        operands.append(moved)
    if reads_coarse:
        operands.append(coarse_moved)

    def kernel(*refs):
        refs = list(refs)
        first, second, _ = refs[:3]
        del refs[:3]
        held = refs.pop(0) if reads_held else None
        arrived = refs.pop(0) if reads_moved else None
        coarse_arrived = refs.pop(0) if reads_coarse else None
        store = refs.pop(0)
        sent = refs.pop(0) if sends_along else None
        coarse_sent = refs.pop(0) if sends_across else None
        state = refs.pop(0)

        index = lax.axis_index("layer")
        position = index & (CF - 1)
        interval = lax.div(index, CF)
        head = position == 0

        def chunk_rows(chunk):
            return pl.ds(pl.multiple_of((chunk * HALVES + half) * part, part), part)

        def fixed_rows(chunk):
            return pl.ds((chunk * HALVES + half) * part, part)

        place = (turn, interval, position)
        never = (index < 0, 0)
        one, chunk = plan.first_pass(*place) if passes_one else never
        two, own = plan.second_pass(*place) if passes_two else never
        chunk = jnp.where(two, own, chunk)
        solving, own = plan.solving(*place) if solves else never
        chunk = jnp.where(solving, own, chunk)
        last, last_chunk = plan.last_pass(*place) if closes else never
        closing = last & ~head
        chunk = jnp.where(closing, last_chunk, chunk)

        if gathers:

            @pl.when(head)
            def _():
                store[FINE, fixed_rows((turn - plan.solve) // 2), :] = arrived[...]

        if reads_held:

            @pl.when(head)
            def _():
                state[...] = held[fixed_rows(turn // 2), :]

        if reads_moved:

            @pl.when((one & ~head) | two | closing)
            def _():
                state[...] = arrived[...]

        if solves:

            @pl.when(solving & (interval == 2))
            def _():
                state[...] = store[FINE, chunk_rows(chunk), :]

        if reads_coarse:

            @pl.when(solving & (interval > 2))
            def _():
                state[...] = coarse_arrived[...] + store[FINE, chunk_rows(chunk), :]

        @pl.when(one | two | closing | solving)
        def _():
            before = state[...]
            change = increment(before, first, second)
            after = before + step * change
            store[PROD, chunk_rows(chunk), :] = after
            if sends_along:
                sent[...] = after
            if passes_two:

                @pl.when(two & head)
                def _():
                    store[PSI, chunk_rows(chunk), :] = before + coarse * change

            if sends_across:

                @pl.when(solving)
                def _():
                    coarse_sent[...] = before + coarse * change - store[PSI, chunk_rows(chunk), :]

        if closes and sends_along:

            @pl.when(last & head)
            def _():
                sent[...] = store[PROD, chunk_rows(last_chunk), :]

    small = pltpu.VMEM((part, width), jnp.float32)
    hidden = first.shape[1]
    results = pl.pallas_call(
        kernel,
        out_shape=(pltpu.VMEM(store.shape, store.dtype),) + (small,) * (sends_along + sends_across),
        in_specs=[VMEM] * len(operands),
        out_specs=(VMEM,) * (1 + sends_along + sends_across),
        scratch_shapes=[small],
        input_output_aliases={2: 0},
        compiler_params=pltpu.CompilerParams(vmem_limit_bytes=8 * 2**20),
        cost_estimate=pl.CostEstimate(
            flops=4 * part * width * hidden, bytes_accessed=4 * width * hidden, transcendentals=part * hidden
        ),
    )(*(in_vmem(x) for x in operands))
    store = results[0]
    moved = lax.ppermute(results[1], "layer", plan.along(turn)) if sends_along else None
    coarse_moved = lax.ppermute(results[-1], "layer", plan.across(turn)) if sends_across else None
    return moved, coarse_moved, store


def body(inputs, w_in, w_out):
    count = lax.axis_size("layer")
    plan = Plan(count // CF)
    step = 1.0 / count
    held, first, second, store = load(inputs, w_in, w_out)
    moved, coarse_moved = [None] * HALVES, [None] * HALVES
    for turn in range(plan.end):
        for half in range(HALVES):
            moved[half], coarse_moved[half], store = stage(
                plan, turn, half, step, CF * step, moved[half], coarse_moved[half], held, first, second, store
            )
    return store[PROD][None]


def solution(mesh):
    return jax.shard_map(
        body,
        mesh=mesh,
        in_specs=(P(), P("layer", None, None), P("layer", None, None)),
        out_specs=P("layer", None, None),
        check_vma=False,
    )
```

```python
import jax
import jax.numpy as jnp
from jax import lax
from jax.experimental import pallas as pl
from jax.experimental.pallas import tpu as pltpu
from jax.sharding import PartitionSpec as P

CF = 8
CHUNKS = 4
HALVES = 2
WINDOW = 6
PIECES = 4
PROD, PSI, FINE = range(3)

VMEM = pl.BlockSpec(memory_space=pltpu.VMEM)
ANY = pl.BlockSpec(memory_space=pl.ANY)


def in_vmem(x):
    return pltpu.with_memory_space_constraint(x, pltpu.VMEM)


def load_kernel(inputs, w_in, w_out, held, first, second, store, sems):
    del store
    copies = [pltpu.make_async_copy(inputs, held, sems.at[0])]
    for source, goal in ((w_in, first), (w_out, second)):
        size = goal.shape[0] // PIECES
        for piece in range(PIECES):
            rows = pl.ds(piece * size, size)
            copies.append(pltpu.make_async_copy(source.at[0, rows], goal.at[rows], sems.at[len(copies)]))
    for copy in copies:
        copy.start()
    for copy in copies:
        copy.wait()


def load(inputs, w_in, w_out):
    rows, width = inputs.shape
    return pl.pallas_call(
        load_kernel,
        out_shape=(
            pltpu.VMEM((rows, width), jnp.float32),
            pltpu.VMEM(w_in.shape[1:], w_in.dtype),
            pltpu.VMEM(w_out.shape[1:], w_out.dtype),
            pltpu.VMEM((3, rows, width), jnp.float32),
        ),
        in_specs=[ANY] * 3,
        out_specs=(VMEM,) * 4,
        scratch_shapes=[pltpu.SemaphoreType.DMA((1 + 2 * PIECES,))],
        compiler_params=pltpu.CompilerParams(vmem_limit_bytes=4 * 2**20),
    )(*(pltpu.with_memory_space_constraint(x, pltpu.HBM) for x in (inputs, w_in, w_out)))


def increment(state, first, second):
    mean_sq = jnp.mean(state * state, axis=-1, keepdims=True)
    hidden = jnp.dot(state.astype(jnp.bfloat16), first[...], preferred_element_type=jnp.float32)
    act = jax.nn.gelu(hidden * lax.rsqrt(mean_sq + 1e-06)).astype(jnp.bfloat16)
    return jnp.dot(act, second[...], preferred_element_type=jnp.float32)


class Plan:
    def __init__(self, points):
        self.points = points
        self.solve = 2 * CF
        self.last = self.solve + points - 3
        self.end = self.last + CF + 2 * CHUNKS - 2

    def chunk(self, turn, start):
        own = turn - start
        return (own >= 0) & (own < 2 * CHUNKS) & (own & 1 == 0), own >> 1

    def first_pass(self, turn, interval, position):
        due, own = self.chunk(turn, position)
        return due & (interval < self.points - 2), own

    def second_pass(self, turn, interval, position):
        due, own = self.chunk(turn, position + CF)
        return due & (interval >= 1) & (interval < self.points - 1), own

    def solving(self, turn, interval, position):
        due, own = self.chunk(turn, self.solve + interval - 2)
        return due & (position == 0) & (interval >= 2), own

    def last_pass(self, turn, interval, position):
        return self.chunk(turn, self.last + position)

    def sends_along(self, turn):
        return turn < self.solve + 2 * CHUNKS - 2 or self.last <= turn < self.end - 1

    def sends_across(self, turn):
        return self.solve <= turn < self.last + 2 * CHUNKS - 2

    def along(self, turn):
        count = CF * self.points
        if CF - 1 <= turn < self.last and turn % 2:
            return [(n, (n + 1) % count) for n in range(count)]
        target = {n: n ^ 1 for n in range(count)}
        if (turn - self.last * (turn >= self.last)) % 2:
            for k in range(self.points):
                for p in range(1, CF - 1, 2):
                    target[CF * k + p] = CF * k + p + 1
                    target[CF * k + p + 1] = CF * k + p
                for p in (0, CF - 1):
                    target[CF * k + p] = CF * (k ^ 1) + p if turn < self.last else CF * k + CF - 1 - p
        return sorted(target.items())

    def across(self, turn):
        start = self.solve + (turn - self.solve) // WINDOW * WINDOW
        target = {n: n ^ 1 for n in range(CF * self.points)}
        for k in range(2, self.points - 1):
            if any(self.solving(t, k, 0)[0] for t in range(start + (turn - start) % 2, start + WINDOW, 2)):
                here, there = CF * k, CF * (k + 1)
                if start + WINDOW <= self.last:
                    target.update({here: there, there: there + 1, there + 1: here + 1, here + 1: here})
                else:
                    target.update({there + p: there + p + 1 for p in range(CF - 1)})
                    target.update({here + p: here + p - 1 for p in range(1, CF)})
                    target.update({here: there, there + CF - 1: here + CF - 1})
        return sorted(target.items())


def stage(plan, turn, half, step, coarse, moved, coarse_moved, held, first, second, store):
    rows, width = held.shape
    part = rows // CHUNKS // HALVES
    sends_along, sends_across = plan.sends_along(turn), plan.sends_across(turn)
    passes_one = turn < CF + 2 * CHUNKS - 2
    passes_two = CF <= turn < 2 * CF + 2 * CHUNKS - 2
    gathers = plan.solve <= turn < plan.solve + 2 * CHUNKS and turn % 2 == 0
    solves = plan.solve <= turn < plan.last + 2 * CHUNKS - 1
    closes = turn >= plan.last
    reads_held = turn < 2 * CHUNKS and turn % 2 == 0
    reads_moved = moved is not None
    reads_coarse = coarse_moved is not None
    operands = [first, second, store]
    if reads_held:
        operands.append(held)
    if reads_moved:
        operands.append(moved)
    if reads_coarse:
        operands.append(coarse_moved)

    def kernel(*refs):
        refs = list(refs)
        first, second, _ = refs[:3]
        del refs[:3]
        held = refs.pop(0) if reads_held else None
        arrived = refs.pop(0) if reads_moved else None
        coarse_arrived = refs.pop(0) if reads_coarse else None
        store = refs.pop(0)
        sent = refs.pop(0) if sends_along else None
        coarse_sent = refs.pop(0) if sends_across else None
        state = refs.pop(0)

        index = lax.axis_index("layer")
        position = index & (CF - 1)
        interval = lax.div(index, CF)
        head = position == 0

        def chunk_rows(chunk):
            return pl.ds(pl.multiple_of((chunk * HALVES + half) * part, part), part)

        def fixed_rows(chunk):
            return pl.ds((chunk * HALVES + half) * part, part)

        place = (turn, interval, position)
        never = (index < 0, 0)
        one, chunk = plan.first_pass(*place) if passes_one else never
        two, own = plan.second_pass(*place) if passes_two else never
        chunk = jnp.where(two, own, chunk)
        solving, own = plan.solving(*place) if solves else never
        chunk = jnp.where(solving, own, chunk)
        last, last_chunk = plan.last_pass(*place) if closes else never
        closing = last & ~head
        chunk = jnp.where(closing, last_chunk, chunk)

        if gathers:

            @pl.when(head)
            def _():
                store[FINE, fixed_rows((turn - plan.solve) // 2), :] = arrived[...]

        if reads_held:

            @pl.when(head)
            def _():
                state[...] = held[fixed_rows(turn // 2), :]

        if reads_moved:

            @pl.when((one & ~head) | two | closing)
            def _():
                state[...] = arrived[...]

        if solves:

            @pl.when(solving & (interval == 2))
            def _():
                state[...] = store[FINE, chunk_rows(chunk), :]

        if reads_coarse:

            @pl.when(solving & (interval > 2))
            def _():
                state[...] = coarse_arrived[...] + store[FINE, chunk_rows(chunk), :]

        @pl.when(one | two | closing | solving)
        def _():
            before = state[...]
            change = increment(before, first, second)
            after = before + step * change
            store[PROD, chunk_rows(chunk), :] = after
            if sends_along:
                sent[...] = after
            if passes_two:

                @pl.when(two & head)
                def _():
                    store[PSI, chunk_rows(chunk), :] = before + coarse * change

            if sends_across:

                @pl.when(solving)
                def _():
                    coarse_sent[...] = before + coarse * change - store[PSI, chunk_rows(chunk), :]

        if closes and sends_along:

            @pl.when(last & head)
            def _():
                sent[...] = store[PROD, chunk_rows(last_chunk), :]

    small = pltpu.VMEM((part, width), jnp.float32)
    hidden = first.shape[1]
    results = pl.pallas_call(
        kernel,
        out_shape=(pltpu.VMEM(store.shape, store.dtype),) + (small,) * (sends_along + sends_across),
        in_specs=[VMEM] * len(operands),
        out_specs=(VMEM,) * (1 + sends_along + sends_across),
        scratch_shapes=[small],
        input_output_aliases={2: 0},
        compiler_params=pltpu.CompilerParams(vmem_limit_bytes=8 * 2**20),
        cost_estimate=pl.CostEstimate(
            flops=4 * part * width * hidden, bytes_accessed=4 * width * hidden, transcendentals=part * hidden
        ),
    )(*(in_vmem(x) for x in operands))
    store = results[0]
    moved = lax.ppermute(results[1], "layer", plan.along(turn)) if sends_along else None
    coarse_moved = lax.ppermute(results[-1], "layer", plan.across(turn)) if sends_across else None
    return moved, coarse_moved, store


def body(inputs, w_in, w_out):
    count = lax.axis_size("layer")
    plan = Plan(count // CF)
    step = 1.0 / count
    held, first, second, store = load(inputs, w_in, w_out)
    moved, coarse_moved = [None] * HALVES, [None] * HALVES
    for turn in range(plan.end):
        for half in range(HALVES):
            moved[half], coarse_moved[half], store = stage(
                plan, turn, half, step, CF * step, moved[half], coarse_moved[half], held, first, second, store
            )
    return store[PROD][None]


def solution(mesh):
    return jax.shard_map(
        body,
        mesh=mesh,
        in_specs=(P(), P("layer", None, None), P("layer", None, None)),
        out_specs=P("layer", None, None),
        check_vma=False,
    )
```

```python
import jax
import jax.numpy as jnp
from jax import lax
from jax.experimental import pallas as pl
from jax.experimental.pallas import tpu as pltpu
from jax.sharding import PartitionSpec as P

CF = 8
CHUNKS = 4
HALVES = 2
WINDOW = 6
PIECES = 4
PROD, PSI, FINE = range(3)

VMEM = pl.BlockSpec(memory_space=pltpu.VMEM)
ANY = pl.BlockSpec(memory_space=pl.ANY)


def in_vmem(x):
    return pltpu.with_memory_space_constraint(x, pltpu.VMEM)


def load_kernel(inputs, w_in, w_out, held, first, second, store, sems):
    del store
    copies = [pltpu.make_async_copy(inputs, held, sems.at[0])]
    for source, goal in ((w_in, first), (w_out, second)):
        size = goal.shape[0] // PIECES
        for piece in range(PIECES):
            rows = pl.ds(piece * size, size)
            copies.append(pltpu.make_async_copy(source.at[0, rows], goal.at[rows], sems.at[len(copies)]))
    for copy in copies:
        copy.start()
    for copy in copies:
        copy.wait()


def load(inputs, w_in, w_out):
    rows, width = inputs.shape
    return pl.pallas_call(
        load_kernel,
        out_shape=(
            pltpu.VMEM((rows, width), jnp.float32),
            pltpu.VMEM(w_in.shape[1:], w_in.dtype),
            pltpu.VMEM(w_out.shape[1:], w_out.dtype),
            pltpu.VMEM((3, rows, width), jnp.float32),
        ),
        in_specs=[ANY] * 3,
        out_specs=(VMEM,) * 4,
        scratch_shapes=[pltpu.SemaphoreType.DMA((1 + 2 * PIECES,))],
        compiler_params=pltpu.CompilerParams(vmem_limit_bytes=4 * 2**20),
    )(*(pltpu.with_memory_space_constraint(x, pltpu.HBM) for x in (inputs, w_in, w_out)))


def increment(state, first, second):
    mean_sq = jnp.mean(state * state, axis=-1, keepdims=True)
    hidden = jnp.dot(state.astype(jnp.bfloat16), first[...], preferred_element_type=jnp.float32)
    act = jax.nn.gelu(hidden * lax.rsqrt(mean_sq + 1e-06)).astype(jnp.bfloat16)
    return jnp.dot(act, second[...], preferred_element_type=jnp.float32)


class Plan:
    def __init__(self, points):
        self.points = points
        self.solve = 2 * CF
        self.last = self.solve + points - 3
        self.end = self.last + CF + 2 * CHUNKS - 2

    def chunk(self, turn, start):
        own = turn - start
        return (own >= 0) & (own < 2 * CHUNKS) & (own & 1 == 0), own >> 1

    def first_pass(self, turn, interval, position):
        due, own = self.chunk(turn, position)
        return due & (interval < self.points - 2), own

    def second_pass(self, turn, interval, position):
        due, own = self.chunk(turn, position + CF)
        return due & (interval >= 1) & (interval < self.points - 1), own

    def solving(self, turn, interval, position):
        due, own = self.chunk(turn, self.solve + interval - 2)
        return due & (position == 0) & (interval >= 2), own

    def last_pass(self, turn, interval, position):
        return self.chunk(turn, self.last + position)

    def sends_along(self, turn):
        return turn < self.solve + 2 * CHUNKS - 2 or self.last <= turn < self.end - 1

    def sends_across(self, turn):
        return self.solve <= turn < self.last + 2 * CHUNKS - 2

    def along(self, turn):
        count = CF * self.points
        if CF - 1 <= turn < self.last and turn % 2:
            return [(n, (n + 1) % count) for n in range(count)]
        target = {n: n ^ 1 for n in range(count)}
        if (turn - self.last * (turn >= self.last)) % 2:
            for k in range(self.points):
                for p in range(1, CF - 1, 2):
                    target[CF * k + p] = CF * k + p + 1
                    target[CF * k + p + 1] = CF * k + p
                for p in (0, CF - 1):
                    target[CF * k + p] = CF * (k ^ 1) + p if turn < self.last else CF * k + CF - 1 - p
        return sorted(target.items())

    def across(self, turn):
        start = self.solve - 2 + (turn - self.solve + 2) // WINDOW * WINDOW
        target = {n: n ^ 1 for n in range(CF * self.points)}
        for k in range(2, self.points - 1):
            if any(self.solving(t, k, 0)[0] for t in range(start + (turn - start) % 2, start + WINDOW, 2)):
                here, there = CF * k, CF * (k + 1)
                if start + WINDOW <= self.last:
                    target.update({here: there, there: there + 1, there + 1: here + 1, here + 1: here})
                else:
                    target.update({there + p: there + p + 1 for p in range(CF - 1)})
                    target.update({here + p: here + p - 1 for p in range(1, CF)})
                    target.update({here: there, there + CF - 1: here + CF - 1})
        return sorted(target.items())


def stage(plan, turn, half, step, coarse, moved, coarse_moved, held, first, second, store):
    rows, width = held.shape
    part = rows // CHUNKS // HALVES
    sends_along, sends_across = plan.sends_along(turn), plan.sends_across(turn)
    passes_one = turn < CF + 2 * CHUNKS - 2
    passes_two = CF <= turn < 2 * CF + 2 * CHUNKS - 2
    gathers = plan.solve <= turn < plan.solve + 2 * CHUNKS and turn % 2 == 0
    solves = plan.solve <= turn < plan.last + 2 * CHUNKS - 1
    closes = turn >= plan.last
    reads_held = turn < 2 * CHUNKS and turn % 2 == 0
    reads_moved = moved is not None
    reads_coarse = coarse_moved is not None
    operands = [first, second, store]
    if reads_held:
        operands.append(held)
    if reads_moved:
        operands.append(moved)
    if reads_coarse:
        operands.append(coarse_moved)

    def kernel(*refs):
        refs = list(refs)
        first, second, _ = refs[:3]
        del refs[:3]
        held = refs.pop(0) if reads_held else None
        arrived = refs.pop(0) if reads_moved else None
        coarse_arrived = refs.pop(0) if reads_coarse else None
        store = refs.pop(0)
        sent = refs.pop(0) if sends_along else None
        coarse_sent = refs.pop(0) if sends_across else None
        state = refs.pop(0)

        index = lax.axis_index("layer")
        position = index & (CF - 1)
        interval = lax.div(index, CF)
        head = position == 0

        def chunk_rows(chunk):
            return pl.ds(pl.multiple_of((chunk * HALVES + half) * part, part), part)

        def fixed_rows(chunk):
            return pl.ds((chunk * HALVES + half) * part, part)

        place = (turn, interval, position)
        never = (index < 0, 0)
        one, chunk = plan.first_pass(*place) if passes_one else never
        two, own = plan.second_pass(*place) if passes_two else never
        chunk = jnp.where(two, own, chunk)
        solving, own = plan.solving(*place) if solves else never
        chunk = jnp.where(solving, own, chunk)
        last, last_chunk = plan.last_pass(*place) if closes else never
        closing = last & ~head
        chunk = jnp.where(closing, last_chunk, chunk)

        if gathers:

            @pl.when(head)
            def _():
                store[FINE, fixed_rows((turn - plan.solve) // 2), :] = arrived[...]

        if reads_held:

            @pl.when(head)
            def _():
                state[...] = held[fixed_rows(turn // 2), :]

        if reads_moved:

            @pl.when((one & ~head) | two | closing)
            def _():
                state[...] = arrived[...]

        if solves:

            @pl.when(solving & (interval == 2))
            def _():
                state[...] = store[FINE, chunk_rows(chunk), :]

        if reads_coarse:

            @pl.when(solving & (interval > 2))
            def _():
                state[...] = coarse_arrived[...] + store[FINE, chunk_rows(chunk), :]

        @pl.when(one | two | closing | solving)
        def _():
            before = state[...]
            change = increment(before, first, second)
            after = before + step * change
            store[PROD, chunk_rows(chunk), :] = after
            if sends_along:
                sent[...] = after
            if passes_two:

                @pl.when(two & head)
                def _():
                    store[PSI, chunk_rows(chunk), :] = before + coarse * change

            if sends_across:

                @pl.when(solving)
                def _():
                    coarse_sent[...] = before + coarse * change - store[PSI, chunk_rows(chunk), :]

        if closes and sends_along:

            @pl.when(last & head)
            def _():
                sent[...] = store[PROD, chunk_rows(last_chunk), :]

    small = pltpu.VMEM((part, width), jnp.float32)
    hidden = first.shape[1]
    results = pl.pallas_call(
        kernel,
        out_shape=(pltpu.VMEM(store.shape, store.dtype),) + (small,) * (sends_along + sends_across),
        in_specs=[VMEM] * len(operands),
        out_specs=(VMEM,) * (1 + sends_along + sends_across),
        scratch_shapes=[small],
        input_output_aliases={2: 0},
        compiler_params=pltpu.CompilerParams(vmem_limit_bytes=8 * 2**20),
        cost_estimate=pl.CostEstimate(
            flops=4 * part * width * hidden, bytes_accessed=4 * width * hidden, transcendentals=part * hidden
        ),
    )(*(in_vmem(x) for x in operands))
    store = results[0]
    moved = lax.ppermute(results[1], "layer", plan.along(turn)) if sends_along else None
    coarse_moved = lax.ppermute(results[-1], "layer", plan.across(turn)) if sends_across else None
    return moved, coarse_moved, store


def body(inputs, w_in, w_out):
    count = lax.axis_size("layer")
    plan = Plan(count // CF)
    step = 1.0 / count
    held, first, second, store = load(inputs, w_in, w_out)
    moved, coarse_moved = [None] * HALVES, [None] * HALVES
    for turn in range(plan.end):
        for half in range(HALVES):
            moved[half], coarse_moved[half], store = stage(
                plan, turn, half, step, CF * step, moved[half], coarse_moved[half], held, first, second, store
            )
    return store[PROD][None]


def solution(mesh):
    return jax.shard_map(
        body,
        mesh=mesh,
        in_specs=(P(), P("layer", None, None), P("layer", None, None)),
        out_specs=P("layer", None, None),
        check_vma=False,
    )
```
